256 devices in a mesh: ctx: 32 (over x_lo, z, core), head: 8 (over x_hi, y).
Axes of the slice: x: 4 (x_hi: 2, x_lo: 2; x = x_hi * 2 + x_lo), y: 4, z: 8, core: 2. Of those that a mesh axis runs over, the one named last changes fastest.
Arguments:
- asking_vectors: bfloat16 [65536, 32, 128], P('ctx', 'head'), as said below
- lookup_vectors: bfloat16 [65536, 32, 128], P('ctx', 'head'), as said below
- content_vectors: bfloat16 [65536, 32, 128], P('ctx', 'head'), may hold values from -6 to 6
- softmax_heat: float32 [32], P('head'), may hold values from 0.02 to 0.2
- document_places: int32 [65536], P('ctx'), may hold values from 0 to 4095, as said below
- digest_shifts: int32 [256, 8], P('ctx'), may hold values from 0 to 255, as said below
Outputs:
- attended: bfloat16 [65536, 32, 128], P(('ctx', 'head'))
The draws below stay inside these ranges and needn't reach their ends.
Inputs may be any that keep to these rules, and one draw needn't show every extreme that they name: `digest_shifts`: the 8 offsets of one stride block are distinct. `document_places`: 0 at a document's first token (the sequence's first token is one) and one more than at the token before otherwise; no document is longer than min(4096, 16384) tokens, and the first one has exactly that length. `asking_vectors`: real-valued entries. `lookup_vectors`: real-valued entries.
All inputs are finite; a program needn't handle non-finite values.
Results may differ from the reference program's by a relative error of at most 0.006.
Values may be sent and summed in bfloat16 or wider, within the bound.
No kernel may reach another device: no remote copies, remote signals or barrier semaphores. Data moves between devices by JAX's collectives and lax.ppermute only.
A program may use at most 128 MiB of HBM per device.

```python
import math
import jax
import jax.numpy as jnp
from jax import lax

ATTENDER_NUMBER = 32
ATTENDER_DIM = 128
STRIDE = 256
SUMM = 8
TOKENS = 65536
STRIDES = 256
SUMMARIES = 2048


def key_field(key):
    shape = (TOKENS, ATTENDER_NUMBER, ATTENDER_DIM)
    field = jnp.clip(jax.random.normal(jax.random.fold_in(key, 11), shape, jnp.float32), -6.0, 6.0)
    return field


def draw_lookup_vectors(key, part):
    field = key_field(key)
    return field.astype(jnp.bfloat16)


def draw_asking_vectors(key, part):
    shape = (TOKENS, ATTENDER_NUMBER, ATTENDER_DIM)
    result = 0.5 * jnp.clip(jax.random.normal(jax.random.fold_in(key, 21), shape, jnp.float32), -6.0, 6.0)
    return result.astype(jnp.bfloat16)


def draw_document_places(key, part):
    token = jnp.arange(TOKENS, dtype=jnp.int32)
    span = min(4096, TOKENS // 4)
    fresh = (jax.random.randint(jax.random.fold_in(key, 31), (TOKENS,), 0, max(span // 2, 2)) == 0) & (token >= span)
    forced = token % span == 0
    starts = jnp.where(fresh | forced, token, 0)
    return (token - lax.cummax(starts, axis=0)).astype(jnp.int32)


def draw_digest_shifts(key, part):
    stride_keys = jax.random.split(jax.random.fold_in(key, 41), STRIDES)

    def one_block(block_key):
        return jax.random.permutation(block_key, STRIDE)[:SUMM]
    return jax.vmap(one_block)(stride_keys).astype(jnp.int32)


def levels(key, dims, shards, smallest, high):
    factor_of = 1.0
    for dim, shards_of in shards:
        steps = jax.random.uniform(jax.random.fold_in(jax.random.fold_in(key, 6), dim), (shards_of,), jnp.float32, smallest / len(shards), high / len(shards))
        factor_of = factor_of * jnp.repeat(jnp.exp(steps), dims[dim] // shards_of).reshape((-1,) + (1,) * (len(dims) - 1 - dim))
    return factor_of


def scatter_about(key, extent, scale, reach, shards=(), held_as=jnp.bfloat16):
    values = scale * jax.random.normal(key, extent, jnp.float32)
    if shards:
        values = values * levels(key, extent, shards, -0.22, 0.18)
    return jnp.clip(values, -reach, reach).astype(held_as)


def setup_inputs(seed: int = 0) -> dict:
    splits = jax.random.split(jax.random.key(seed), 7)
    return {
        "asking_vectors": draw_asking_vectors(jax.random.fold_in(splits[6], 71), 0),
        "lookup_vectors": draw_lookup_vectors(jax.random.fold_in(splits[6], 71), 0),
        "content_vectors": scatter_about(splits[2], (TOKENS, ATTENDER_NUMBER, ATTENDER_DIM), 1.0, 6.0, ((0, 32), (1, 8))),
        "softmax_heat": jnp.clip(jnp.exp(math.log(0.2) - 2.3025851 * jax.random.uniform(splits[3], (ATTENDER_NUMBER,), jnp.float32) ** levels(splits[3], (ATTENDER_NUMBER,), ((0, 8),), -0.2, 0.2)), 0.02, 0.2),
        "document_places": draw_document_places(jax.random.fold_in(splits[6], 71), 0),
        "digest_shifts": draw_digest_shifts(jax.random.fold_in(splits[6], 71), 0),
    }


def reference(asking_vectors, lookup_vectors, content_vectors, softmax_heat, document_places, digest_shifts):
    summary_rows = (jnp.arange(STRIDES, dtype=jnp.int32)[:, None] * STRIDE + digest_shifts).reshape(-1).astype(jnp.int32)
    summary_keys = lookup_vectors[summary_rows].astype(jnp.float32)
    summary_values = content_vectors[summary_rows].astype(jnp.float32)
    summary_stride = jnp.arange(SUMMARIES, dtype=jnp.int32) // SUMM
    log_of_place = jnp.log(1.0 + document_places.astype(jnp.float32))
    energy_multiplier = (1.0 + softmax_heat[None, :] * log_of_place[:, None]) / math.sqrt(ATTENDER_DIM)
    inner_pos = jnp.arange(STRIDE, dtype=jnp.int32)
    causal = inner_pos[:, None] >= inner_pos[None, :]

    def one_stride(band_stride_index):
        start_row = (band_stride_index * STRIDE).astype(jnp.int32)
        query_block = lax.dynamic_slice_in_dim(asking_vectors, start_row, STRIDE, 0).astype(jnp.float32)
        key_block = lax.dynamic_slice_in_dim(lookup_vectors, start_row, STRIDE, 0).astype(jnp.float32)
        value_block = lax.dynamic_slice_in_dim(content_vectors, start_row, STRIDE, 0).astype(jnp.float32)
        scale_block = lax.dynamic_slice_in_dim(energy_multiplier, start_row, STRIDE, 0).T
        band_scores = jnp.einsum('qhd,khd->hqk', query_block, key_block) * scale_block[:, :, None]
        band_scores = jnp.where(causal[None], band_scores, -jnp.inf)
        summary_scores = jnp.einsum('qhd,shd->hqs', query_block, summary_keys) * scale_block[:, :, None]
        visible = summary_stride < band_stride_index
        summary_scores = jnp.where(visible[None, None, :], summary_scores, -jnp.inf)
        top_score = jnp.maximum(band_scores.max(-1), summary_scores.max(-1))
        band_weight = jnp.exp(band_scores - top_score[:, :, None])
        summary_column_weight = jnp.exp(summary_scores - top_score[:, :, None])
        total_weight = band_weight.sum(-1) + summary_column_weight.sum(-1)
        band_prob = band_weight.astype(jnp.bfloat16).astype(jnp.float32)
        summary_prob = summary_column_weight.astype(jnp.bfloat16).astype(jnp.float32)
        numerator = jnp.einsum('hqk,khd->qhd', band_prob, value_block)
        numerator = numerator + jnp.einsum('hqs,shd->qhd', summary_prob, summary_values)
        return (numerator / total_weight.T[:, :, None]).astype(jnp.bfloat16)
    attended = lax.map(one_stride, jnp.arange(STRIDES, dtype=jnp.int32))
    return attended.reshape(TOKENS, ATTENDER_NUMBER, ATTENDER_DIM)
```

```python
import functools
import math

import jax
import jax.numpy as jnp
from jax import lax
from jax.experimental import pallas as pl
from jax.experimental.pallas import tpu as pltpu
from jax.sharding import Mesh
from jax.sharding import PartitionSpec as P

F32, BF16 = jnp.float32, jnp.bfloat16
NEG = -1e30
STRIDE, SUMM, DIM, HEADS = 256, 8, 128, 4
BLOCKS = 8
COLS = BLOCKS * SUMM
CHIPS = 8
GROUP = 2
TRANS_B = (((1,), (1,)), ((), ()))
CTX = ("x_lo", "z", "core")
HEAD = ("x_hi", "y")


def gather_kernel(shift_ref, k_hbm, v_hbm, out0_ref, out1_ref, rows_ref, wide_ref, sems):
    for w, hbm in enumerate((k_hbm, v_hbm)):
        for c in range(COLS):
            row = (c // SUMM) * STRIDE + shift_ref[c // SUMM, c % SUMM]
            pltpu.make_async_copy(
                hbm.at[pl.ds(row, 1)], rows_ref.at[w, pl.ds(c, 1)], sems.at[w]
            ).start()
    for w, hbm in enumerate((k_hbm, v_hbm)):
        pltpu.make_async_copy(hbm.at[pl.ds(0, COLS)], rows_ref.at[w], sems.at[w]).wait()
        for c in range(COLS):
            wide_ref[w, pl.ds(c * HEADS, HEADS), :] = rows_ref[w, c].astype(F32)
        for h in range(HEADS):
            out_ref = (out0_ref, out1_ref)[h // GROUP]
            x = wide_ref[w, pl.ds(h, COLS, stride=HEADS), :].astype(BF16)
            for d in range(CHIPS):
                out_ref[d, w, h % GROUP] = x


def gather_summaries(digest_shifts, keys, values):
    out = jax.ShapeDtypeStruct((CHIPS, 2, GROUP, COLS, DIM), BF16)
    return pl.pallas_call(
        gather_kernel,
        in_specs=[
            pl.BlockSpec(memory_space=pltpu.SMEM),
            pl.BlockSpec(memory_space=pl.ANY),
            pl.BlockSpec(memory_space=pl.ANY),
        ],
        out_shape=[out, out],
        scratch_shapes=[
            pltpu.VMEM((2, COLS, HEADS, DIM), BF16),
            pltpu.VMEM((2, COLS * HEADS, DIM), F32),
            pltpu.SemaphoreType.DMA((2,)),
        ],
        name="gather_summaries",
    )(digest_shifts, keys, values)


def attend(q, keys, values, biases, m, l, acc):
    scores = []
    for k, bias in zip(keys, biases):
        s = lax.dot_general(
            q, jnp.concatenate([k, k], axis=1), TRANS_B, preferred_element_type=F32
        )
        scores.append(s if bias is None else s + bias)
    top = m
    for s in scores:
        peak = s.max(axis=1, keepdims=True)
        top = peak if top is None else jnp.maximum(top, peak)
    if m is not None:
        shrink = jnp.exp2(m - top)
        acc, l = acc * shrink, l * shrink
    for s, v in zip(scores, values):
        p = jnp.exp2(s - top).astype(BF16)
        o = jnp.dot(
            p, jnp.concatenate([v, jnp.ones_like(v)], axis=1), preferred_element_type=F32
        )
        acc = o[:, :DIM] if acc is None else acc + o[:, :DIM]
        l = o[:, DIM:] if l is None else l + o[:, DIM:]
    return top, l, acc


def pack_stats(m, l):
    lane = lax.broadcasted_iota(jnp.int32, l.shape, 1)
    return jnp.where(lane < DIM // 2, m, l)


def unpack_stats(ml):
    return ml[:, 0:1], jnp.broadcast_to(ml[:, DIM // 2 : DIM // 2 + 1], ml.shape)


def band_kernel(heat_ref, place_ref, q_ref, k_ref, v_ref, qs_ref, acc_ref, ml_ref, wide_ref):
    j = pl.program_id(0)
    place = place_ref[pl.ds(j, 1), :].astype(F32)
    log_place = jnp.broadcast_to(jnp.log(1.0 + place), (8, STRIDE))
    scale = (1.0 + heat_ref[...] * log_place) * (math.log2(math.e) / math.sqrt(DIM))
    scale = scale.T
    for w, ref in enumerate((q_ref, k_ref, v_ref)):
        wide_ref[w] = ref[...].astype(F32)
    inner = [lax.broadcasted_iota(jnp.int32, (STRIDE, STRIDE), d) for d in range(2)]
    bias = jnp.where(inner[0] >= inner[1], 0.0, NEG)
    for h in range(HEADS):
        q, k, v = (wide_ref[w, pl.ds(h, STRIDE, stride=HEADS), :] for w in range(3))
        q = q * scale[:, h : h + 1]
        high = q.astype(BF16)
        low = (q - high.astype(F32)).astype(BF16)
        q = jnp.concatenate([high, low], axis=1)
        m, l, acc = attend(q, (k.astype(BF16),), (v.astype(BF16),), (bias,), None, None, None)
        qs_ref[h] = q
        acc_ref[h] = acc
        ml_ref[h] = pack_stats(m, l)


def band(heat, places, q, k, v):
    tokens = BLOCKS * STRIDE
    whole = lambda *s: pl.BlockSpec(s, lambda j: (0,) * len(s))
    rows = pl.BlockSpec((STRIDE * HEADS, DIM), lambda j: (j, 0))
    out = lambda d: pl.BlockSpec((HEADS, STRIDE, d), lambda j: (0, j, 0))
    shape = lambda d, t: jax.ShapeDtypeStruct((HEADS, tokens, d), t)
    return pl.pallas_call(
        band_kernel,
        grid=(BLOCKS,),
        in_specs=[whole(8, 1), whole(BLOCKS, STRIDE), rows, rows, rows],
        out_specs=[out(2 * DIM), out(DIM), out(DIM)],
        out_shape=[shape(2 * DIM, BF16), shape(DIM, F32), shape(DIM, F32)],
        scratch_shapes=[pltpu.VMEM((3, STRIDE * HEADS, DIM), F32)],
        compiler_params=pltpu.CompilerParams(vmem_limit_bytes=32 << 20),
        cost_estimate=pl.CostEstimate(
            flops=4 * HEADS * tokens * STRIDE * DIM * 2, bytes_accessed=20 << 20,
            transcendentals=HEADS * tokens * STRIDE,
        ),
        name="band",
    )(heat, places, q, k, v)


def own_kernel(at_ref, q_ref, km_ref, ko_ref, vm_ref, vo_ref, acc_ref, ml_ref, acc_out, ml_out):
    z, core = at_ref[1], at_ref[2]
    flat = lambda ref: ref[...].reshape(CHIPS * COLS, DIM)
    keys, values = (flat(km_ref), flat(ko_ref)), (flat(vm_ref), flat(vo_ref))
    col = lax.broadcasted_iota(jnp.int32, (1, CHIPS * COLS), 1)
    other = jnp.where(col < (z + core) * COLS, 0.0, NEG)
    for j in range(BLOCKS):
        rows = pl.ds(j * STRIDE, STRIDE)
        mine = jnp.where(col < z * COLS + SUMM * j, 0.0, NEG)
        m, l = unpack_stats(ml_ref[0, rows, :])
        m, l, acc = attend(q_ref[0, rows, :], keys, values, (mine, other), m, l, acc_ref[0, rows, :])
        acc_out[0, rows, :] = acc
        ml_out[0, rows, :] = pack_stats(m, l)


def far_kernel(at_ref, q_ref, km_ref, ko_ref, vm_ref, vo_ref, acc_ref, ml_ref, out_ref):
    x = at_ref[0]

    @pl.when(x == 1)
    def _():
        flat = lambda ref: ref[...].reshape(CHIPS * COLS, DIM)
        keys, values = (flat(km_ref), flat(ko_ref)), (flat(vm_ref), flat(vo_ref))
        for j in range(BLOCKS):
            rows = pl.ds(j * STRIDE, STRIDE)
            m, l = unpack_stats(ml_ref[0, rows, :])
            m, l, acc = attend(
                q_ref[0, rows, :], keys, values, (None, None), m, l, acc_ref[0, rows, :]
            )
            out_ref[j, 0] = (acc / l).astype(BF16)

    @pl.when(x == 0)
    def _():
        for j in range(BLOCKS):
            rows = pl.ds(j * STRIDE, STRIDE)
            _, l = unpack_stats(ml_ref[0, rows, :])
            out_ref[j, 0] = (acc_ref[0, rows, :] / l).astype(BF16)


def summaries(kernel, at, q, mine, other, acc, ml, group, name, out_specs, out_shape):
    tokens = BLOCKS * STRIDE
    first = group * GROUP
    kv = lambda w: pl.BlockSpec((CHIPS, 1, 1, COLS, DIM), lambda h: (0, w, h, 0, 0))
    state = lambda d, at=0: pl.BlockSpec((1, tokens, d), lambda h: (h + at, 0, 0))
    shift = first if acc.shape[0] == HEADS else 0
    return pl.pallas_call(
        kernel,
        grid=(GROUP,),
        in_specs=[
            pl.BlockSpec(memory_space=pltpu.SMEM),
            state(2 * DIM, first),
            kv(0), kv(0), kv(1), kv(1),
            state(DIM, shift), state(DIM, shift),
        ],
        out_specs=out_specs,
        out_shape=out_shape,
        compiler_params=pltpu.CompilerParams(vmem_limit_bytes=48 << 20),
        cost_estimate=pl.CostEstimate(
            flops=4 * GROUP * tokens * 2 * CHIPS * COLS * DIM * 2, bytes_accessed=12 << 20,
            transcendentals=GROUP * tokens * 2 * CHIPS * COLS,
        ),
        name=name,
    )(at, q, mine, other, mine, other, acc, ml)


def own_summaries(at, q, mine, other, acc, ml, group):
    tokens = BLOCKS * STRIDE
    spec = pl.BlockSpec((1, tokens, DIM), lambda h: (h, 0, 0))
    shape = jax.ShapeDtypeStruct((GROUP, tokens, DIM), F32)
    return summaries(
        own_kernel, at, q, mine, other, acc, ml, group, f"own_{group}", [spec] * 2, [shape] * 2
    )


def far_summaries(at, q, mine, other, acc, ml, group):
    spec = pl.BlockSpec((BLOCKS, 1, STRIDE, DIM), lambda h: (0, h, 0, 0))
    shape = jax.ShapeDtypeStruct((BLOCKS, GROUP, STRIDE, DIM), BF16)
    return summaries(far_kernel, at, q, mine, other, acc, ml, group, f"far_{group}", spec, shape)


def assemble_kernel(x0_ref, x1_ref, out_ref, wide_ref):
    count = x0_ref.shape[2]
    total = BLOCKS * HEADS
    for source in range(BLOCKS):
        for h in range(HEADS):
            ref = (x0_ref, x1_ref)[h // GROUP]
            wide_ref[pl.ds(source * HEADS + h, count, stride=total), :] = ref[
                source, h % GROUP
            ].astype(F32)
    out_ref[...] = wide_ref[...].astype(BF16)


def assemble(x0, x1, steps=4):
    count = STRIDE // steps
    total = BLOCKS * HEADS
    spec = pl.BlockSpec((BLOCKS, GROUP, count, DIM), lambda t: (0, 0, t, 0))
    return pl.pallas_call(
        assemble_kernel,
        grid=(steps,),
        in_specs=[spec, spec],
        out_specs=pl.BlockSpec((count * total, DIM), lambda t: (t, 0)),
        out_shape=jax.ShapeDtypeStruct((STRIDE * total, DIM), BF16),
        scratch_shapes=[pltpu.VMEM((count * total, DIM), F32)],
        name="assemble",
    )(x0, x1)


def per_device(q, k, v, heat, places, shifts):
    at = jnp.stack([lax.axis_index(a) for a in CTX]).astype(jnp.int32)
    tokens = BLOCKS * STRIDE
    sends = gather_summaries(shifts, k, v)
    mine = [lax.all_to_all(s, "z", 0, 0, tiled=True) for s in sends]
    heat8 = jnp.pad(heat, (0, 8 - HEADS)).reshape(8, 1)
    flat = lambda x: x.reshape(tokens * HEADS, DIM)
    qs, acc, ml = band(heat8, places.reshape(BLOCKS, STRIDE), flat(q), flat(k), flat(v))
    swap = [(0, 1), (1, 0)]
    mine[0], mine[1], qs, acc, ml = lax.optimization_barrier((mine[0], mine[1], qs, acc, ml))
    parts = []
    for g in range(2):
        other = lax.ppermute(mine[g], "core", swap)
        far_mine = lax.ppermute(mine[g], "x_lo", [(0, 1)])
        far_other = lax.ppermute(far_mine, "core", swap)
        acc_g, ml_g = own_summaries(at, qs, mine[g], other, acc, ml, g)
        out = far_summaries(at, qs, far_mine, far_other, acc_g, ml_g, g)
        parts.append(lax.all_to_all(out, HEAD, 0, 0, tiled=True))
    return assemble(*parts).reshape(STRIDE, BLOCKS * HEADS, DIM)


def solution(mesh):
    devices = mesh.devices
    wide = Mesh(devices.reshape(2, 8, 2, 2, 4), CTX + HEAD)
    in_specs = (
        P(CTX, HEAD, None),
        P(CTX, HEAD, None),
        P(CTX, HEAD, None),
        P(HEAD),
        P(CTX),
        P(CTX, None),
    )
    return jax.shard_map(
        per_device, mesh=wide, in_specs=in_specs, out_specs=P(CTX + HEAD, None, None),
        check_vma=False,
    )
```

```python
import functools
import math

import jax
import jax.numpy as jnp
from jax import lax
from jax.experimental import pallas as pl
from jax.experimental.pallas import tpu as pltpu
from jax.sharding import Mesh
from jax.sharding import PartitionSpec as P

F32, BF16 = jnp.float32, jnp.bfloat16
NEG = -1e30
STRIDE, SUMM, DIM, HEADS = 256, 8, 128, 4
BLOCKS = 8
COLS = BLOCKS * SUMM
CHIPS = 8
GROUP = 2
TRANS_B = (((1,), (1,)), ((), ()))
CTX = ("x_lo", "z", "core")
HEAD = ("x_hi", "y")


def gather_kernel(shift_ref, k_hbm, v_hbm, out0_ref, out1_ref, rows_ref, wide_ref, sems):
    for w, hbm in enumerate((k_hbm, v_hbm)):
        for c in range(COLS):
            row = (c // SUMM) * STRIDE + shift_ref[c // SUMM, c % SUMM]
            pltpu.make_async_copy(
                hbm.at[pl.ds(row, 1)], rows_ref.at[w, pl.ds(c, 1)], sems.at[w]
            ).start()
    for w, hbm in enumerate((k_hbm, v_hbm)):
        pltpu.make_async_copy(hbm.at[pl.ds(0, COLS)], rows_ref.at[w], sems.at[w]).wait()
        for c in range(COLS):
            wide_ref[w, pl.ds(c * HEADS, HEADS), :] = rows_ref[w, c].astype(F32)
        for h in range(HEADS):
            out_ref = (out0_ref, out1_ref)[h // GROUP]
            x = wide_ref[w, pl.ds(h, COLS, stride=HEADS), :].astype(BF16)
            for d in range(CHIPS):
                out_ref[d, w, h % GROUP] = x


def gather_summaries(digest_shifts, keys, values):
    out = jax.ShapeDtypeStruct((CHIPS, 2, GROUP, COLS, DIM), BF16)
    return pl.pallas_call(
        gather_kernel,
        in_specs=[
            pl.BlockSpec(memory_space=pltpu.SMEM),
            pl.BlockSpec(memory_space=pl.ANY),
            pl.BlockSpec(memory_space=pl.ANY),
        ],
        out_shape=[out, out],
        scratch_shapes=[
            pltpu.VMEM((2, COLS, HEADS, DIM), BF16),
            pltpu.VMEM((2, COLS * HEADS, DIM), F32),
            pltpu.SemaphoreType.DMA((2,)),
        ],
        name="gather_summaries",
    )(digest_shifts, keys, values)


def attend(q, keys, values, biases, m, l, acc):
    scores = []
    for k, bias in zip(keys, biases):
        s = lax.dot_general(
            q, jnp.concatenate([k, k], axis=1), TRANS_B, preferred_element_type=F32
        )
        scores.append(s if bias is None else s + bias)
    top = m
    for s in scores:
        peak = s.max(axis=1, keepdims=True)
        top = peak if top is None else jnp.maximum(top, peak)
    if m is not None:
        shrink = jnp.exp2(m - top)
        acc, l = acc * shrink, l * shrink
    for s, v in zip(scores, values):
        p = jnp.exp2(s - top).astype(BF16)
        o = jnp.dot(
            p, jnp.concatenate([v, jnp.ones_like(v)], axis=1), preferred_element_type=F32
        )
        acc = o[:, :DIM] if acc is None else acc + o[:, :DIM]
        l = o[:, DIM:] if l is None else l + o[:, DIM:]
    return top, l, acc


def pack_stats(m, l):
    lane = lax.broadcasted_iota(jnp.int32, l.shape, 1)
    return jnp.where(lane < DIM // 2, m, l)


def unpack_stats(ml):
    return ml[:, 0:1], jnp.broadcast_to(ml[:, DIM // 2 : DIM // 2 + 1], ml.shape)


def band_kernel(heat_ref, place_ref, q_ref, k_ref, v_ref, *refs):
    *outs, wide_ref = refs
    j = pl.program_id(0)
    place = place_ref[pl.ds(j, 1), :].astype(F32)
    log_place = jnp.broadcast_to(jnp.log(1.0 + place), (8, STRIDE))
    scale = (1.0 + heat_ref[...] * log_place) * (math.log2(math.e) / math.sqrt(DIM))
    scale = scale.T
    for w, ref in enumerate((q_ref, k_ref, v_ref)):
        wide_ref[w] = ref[...].astype(F32)
    inner = [lax.broadcasted_iota(jnp.int32, (STRIDE, STRIDE), d) for d in range(2)]
    bias = jnp.where(inner[0] >= inner[1], 0.0, NEG)
    for h in range(HEADS):
        q, k, v = (wide_ref[w, pl.ds(h, STRIDE, stride=HEADS), :] for w in range(3))
        q = q * scale[:, h : h + 1]
        high = q.astype(BF16)
        low = (q - high.astype(F32)).astype(BF16)
        q = jnp.concatenate([high, low], axis=1)
        m, l, acc = attend(q, (k.astype(BF16),), (v.astype(BF16),), (bias,), None, None, None)
        qs_ref, acc_ref, ml_ref = outs[3 * (h // GROUP) :][:3]
        qs_ref[h % GROUP] = q
        acc_ref[h % GROUP] = acc
        ml_ref[h % GROUP] = pack_stats(m, l)


def band(heat, places, q, k, v):
    tokens = BLOCKS * STRIDE
    whole = lambda *s: pl.BlockSpec(s, lambda j: (0,) * len(s))
    rows = pl.BlockSpec((STRIDE * HEADS, DIM), lambda j: (j, 0))
    out = lambda d: pl.BlockSpec((GROUP, STRIDE, d), lambda j: (0, j, 0))
    shape = lambda d, t: jax.ShapeDtypeStruct((GROUP, tokens, d), t)
    return pl.pallas_call(
        band_kernel,
        grid=(BLOCKS,),
        in_specs=[whole(8, 1), whole(BLOCKS, STRIDE), rows, rows, rows],
        out_specs=[out(2 * DIM), out(DIM), out(DIM)] * 2,
        out_shape=[shape(2 * DIM, BF16), shape(DIM, F32), shape(DIM, F32)] * 2,
        scratch_shapes=[pltpu.VMEM((3, STRIDE * HEADS, DIM), F32)],
        compiler_params=pltpu.CompilerParams(vmem_limit_bytes=60 << 20),
        cost_estimate=pl.CostEstimate(
            flops=4 * HEADS * tokens * STRIDE * DIM * 2, bytes_accessed=20 << 20,
            transcendentals=HEADS * tokens * STRIDE,
        ),
        name="band",
    )(heat, places, q, k, v)


def attend_blocks(q_ref, kv_refs, biases, acc_ref, ml_ref, put):
    flat = lambda ref: ref[...].reshape(CHIPS * COLS, DIM)
    keys = [flat(k) for k, _ in kv_refs]
    values = [flat(v) for _, v in kv_refs]
    for j in range(BLOCKS):
        rows = pl.ds(j * STRIDE, STRIDE)
        m, l = unpack_stats(ml_ref[0, rows, :])
        put(j, *attend(q_ref[0, rows, :], keys, values, biases(j), m, l, acc_ref[0, rows, :]))


def own_biases(at_ref):
    z, core = at_ref[1], at_ref[2]
    col = lax.broadcasted_iota(jnp.int32, (1, CHIPS * COLS), 1)
    other = jnp.where(col < (z + core) * COLS, 0.0, NEG)
    return lambda j: [jnp.where(col < z * COLS + SUMM * j, 0.0, NEG), other]


def no_biases(j):
    return [None, None]


def summary_kernel(own, far, at_ref, q_ref, *refs):
    kv_refs, refs = refs[: 4 * (own + far)], refs[4 * (own + far) :]
    acc_ref, ml_ref, *outs = refs
    kv = [(kv_refs[i], kv_refs[i + 2]) for s in range(own + far) for i in (4 * s, 4 * s + 1)]

    def keep(j, m, l, acc):
        rows = pl.ds(j * STRIDE, STRIDE)
        outs[0][0, rows, :] = acc
        outs[1][0, rows, :] = pack_stats(m, l)

    def finish(j, m, l, acc):
        outs[0][j, 0] = (acc / l).astype(BF16)

    if not far:
        attend_blocks(q_ref, kv, own_biases(at_ref), acc_ref, ml_ref, keep)
        return

    @pl.when(at_ref[0] == 1)
    def _():
        near = own_biases(at_ref) if own else lambda j: []
        attend_blocks(q_ref, kv, lambda j: near(j) + [None, None], acc_ref, ml_ref, finish)

    @pl.when(at_ref[0] == 0)
    def _():
        if own:
            attend_blocks(q_ref, kv[:2], own_biases(at_ref), acc_ref, ml_ref, finish)
        else:
            for j in range(BLOCKS):
                rows = pl.ds(j * STRIDE, STRIDE)
                m, l = unpack_stats(ml_ref[0, rows, :])
                finish(j, m, l, acc_ref[0, rows, :])


def summaries(at, q, acc, ml, own=(), far=()):
    tokens = BLOCKS * STRIDE
    kv = lambda w: pl.BlockSpec((CHIPS, 1, 1, COLS, DIM), lambda h: (0, w, h, 0, 0))
    state = lambda d: pl.BlockSpec((1, tokens, d), lambda h: (h, 0, 0))
    sets = [s for s in (own, far) if s]
    if far:
        out_specs = pl.BlockSpec((BLOCKS, 1, STRIDE, DIM), lambda h: (0, h, 0, 0))
        out_shape = jax.ShapeDtypeStruct((BLOCKS, GROUP, STRIDE, DIM), BF16)
    else:
        out_specs = [state(DIM)] * 2
        out_shape = [jax.ShapeDtypeStruct((GROUP, tokens, DIM), F32)] * 2
    work = GROUP * tokens * 2 * CHIPS * COLS * len(sets)
    return pl.pallas_call(
        functools.partial(summary_kernel, bool(own), bool(far)),
        grid=(GROUP,),
        in_specs=[
            pl.BlockSpec(memory_space=pltpu.SMEM),
            state(2 * DIM),
            *[kv(0), kv(0), kv(1), kv(1)] * len(sets),
            state(DIM), state(DIM),
        ],
        out_specs=out_specs,
        out_shape=out_shape,
        compiler_params=pltpu.CompilerParams(vmem_limit_bytes=60 << 20),
        cost_estimate=pl.CostEstimate(
            flops=8 * work * DIM, bytes_accessed=12 << 20, transcendentals=work
        ),
        name="_".join(n for n, s in (("own", own), ("far", far)) if s),
    )(at, q, *[x for mine, other in sets for x in (mine, other) * 2], acc, ml)


def assemble_kernel(x0_ref, x1_ref, out_ref):
    heads = [(x0_ref, x1_ref)[h // GROUP][s, h % GROUP] for s in range(BLOCKS) for h in range(HEADS)]
    out_ref[...] = jnp.swapaxes(jnp.stack(heads), 0, 1)


def assemble(x0, x1, steps=4):
    count = STRIDE // steps
    total = BLOCKS * HEADS
    spec = pl.BlockSpec((BLOCKS, GROUP, count, DIM), lambda t: (0, 0, t, 0))
    return pl.pallas_call(
        assemble_kernel,
        grid=(steps,),
        in_specs=[spec, spec],
        out_specs=pl.BlockSpec((count, total, DIM), lambda t: (t, 0, 0)),
        out_shape=jax.ShapeDtypeStruct((STRIDE, total, DIM), BF16),
        compiler_params=pltpu.CompilerParams(vmem_limit_bytes=60 << 20),
        name="assemble",
    )(x0, x1)


def after(value, *done):
    return lax.optimization_barrier((value, *done))[0]


def per_device(q, k, v, heat, places, shifts):
    at = jnp.stack([lax.axis_index(a) for a in CTX]).astype(jnp.int32)
    tokens = BLOCKS * STRIDE
    swap, up = [(0, 1), (1, 0)], [(0, 1)]
    flat = lambda x: x.reshape(tokens * HEADS, DIM)
    spread = lambda x: lax.all_to_all(x, "z", 0, 0, tiled=True)
    give = lambda x: lax.all_to_all(x, HEAD, 0, 0, tiled=True)
    heat8 = jnp.pad(heat, (0, 8 - HEADS)).reshape(8, 1)

    send0, send1 = gather_summaries(shifts, k, v)
    mine0 = spread(send0)
    qs0, acc0, ml0, qs1, acc1, ml1 = band(heat8, places.reshape(BLOCKS, STRIDE), flat(q), flat(k), flat(v))
    mine0 = after(mine0, ml0)
    mine1 = spread(after(send1, mine0))
    other0 = lax.ppermute(mine0, "core", swap)
    far0 = lax.ppermute(mine0, "x_lo", up)
    state0 = summaries(at, qs0, acc0, ml0, own=(mine0, other0))
    far0 = after(far0, state0[1])
    far_other0 = lax.ppermute(far0, "core", swap)
    mine1 = after(mine1, state0[1])
    other1 = lax.ppermute(mine1, "core", swap)
    far1 = lax.ppermute(mine1, "x_lo", up)
    part0 = summaries(at, qs0, *state0, far=(far0, far_other0))
    out0 = give(part0)
    far1 = after(far1, part0)
    far_other1 = lax.ppermute(far1, "core", swap)
    acc1 = after(acc1, part0)
    part1 = summaries(at, qs1, acc1, ml1, own=(mine1, other1), far=(far1, far_other1))
    out1 = give(after(part1, out0))
    return assemble(out0, out1)


def solution(mesh):
    devices = mesh.devices
    wide = Mesh(devices.reshape(2, 8, 2, 2, 4), CTX + HEAD)
    in_specs = (
        P(CTX, HEAD, None),
        P(CTX, HEAD, None),
        P(CTX, HEAD, None),
        P(HEAD),
        P(CTX),
        P(CTX, None),
    )
    return jax.shard_map(
        per_device, mesh=wide, in_specs=in_specs, out_specs=P(CTX + HEAD, None, None),
        check_vma=False,
    )
```

```python
import functools
import math

import jax
import jax.numpy as jnp
from jax import lax
from jax.experimental import pallas as pl
from jax.experimental.pallas import tpu as pltpu
from jax.sharding import Mesh
from jax.sharding import PartitionSpec as P

F32, BF16 = jnp.float32, jnp.bfloat16
NEG = -1e30
STRIDE, SUMM, DIM, HEADS = 256, 8, 128, 4
BLOCKS = 8
COLS = BLOCKS * SUMM
CHIPS = 8
GROUP = 2
TRANS_B = (((1,), (1,)), ((), ()))
CTX = ("x_lo", "z", "core")
HEAD = ("x_hi", "y")


def gather_kernel(shift_ref, k_hbm, v_hbm, out0_ref, out1_ref, rows_ref, wide_ref, sems):
    for w, hbm in enumerate((k_hbm, v_hbm)):
        for c in range(COLS):
            row = (c // SUMM) * STRIDE + shift_ref[c // SUMM, c % SUMM]
            pltpu.make_async_copy(
                hbm.at[pl.ds(row, 1)], rows_ref.at[w, pl.ds(c, 1)], sems.at[w]
            ).start()
    for w, hbm in enumerate((k_hbm, v_hbm)):
        pltpu.make_async_copy(hbm.at[pl.ds(0, COLS)], rows_ref.at[w], sems.at[w]).wait()
        for c in range(COLS):
            wide_ref[w, pl.ds(c * HEADS, HEADS), :] = rows_ref[w, c].astype(F32)
        for h in range(HEADS):
            out_ref = (out0_ref, out1_ref)[h // GROUP]
            x = wide_ref[w, pl.ds(h, COLS, stride=HEADS), :].astype(BF16)
            for d in range(CHIPS):
                out_ref[d, w, h % GROUP] = x


def gather_summaries(digest_shifts, keys, values):
    out = jax.ShapeDtypeStruct((CHIPS, 2, GROUP, COLS, DIM), BF16)
    return pl.pallas_call(
        gather_kernel,
        in_specs=[
            pl.BlockSpec(memory_space=pltpu.SMEM),
            pl.BlockSpec(memory_space=pl.ANY),
            pl.BlockSpec(memory_space=pl.ANY),
        ],
        out_shape=[out, out],
        scratch_shapes=[
            pltpu.VMEM((2, COLS, HEADS, DIM), BF16),
            pltpu.VMEM((2, COLS * HEADS, DIM), F32),
            pltpu.SemaphoreType.DMA((2,)),
        ],
        name="gather_summaries",
    )(digest_shifts, keys, values)


def attend(q, keys, values, biases, m, l, acc):
    scores = []
    for k, bias in zip(keys, biases):
        s = lax.dot_general(
            q, jnp.concatenate([k, k], axis=1), TRANS_B, preferred_element_type=F32
        )
        scores.append(s if bias is None else s + bias)
    top = m
    for s in scores:
        peak = s.max(axis=1, keepdims=True)
        top = peak if top is None else jnp.maximum(top, peak)
    if m is not None:
        shrink = jnp.exp2(m - top)
        acc, l = acc * shrink, l * shrink
    for s, v in zip(scores, values):
        p = jnp.exp2(s - top).astype(BF16)
        o = jnp.dot(
            p, jnp.concatenate([v, jnp.ones_like(v)], axis=1), preferred_element_type=F32
        )
        acc = o[:, :DIM] if acc is None else acc + o[:, :DIM]
        l = o[:, DIM:] if l is None else l + o[:, DIM:]
    return top, l, acc


def pack_stats(m, l):
    lane = lax.broadcasted_iota(jnp.int32, l.shape, 1)
    return jnp.where(lane < DIM // 2, m, l)


def unpack_stats(ml):
    return ml[:, 0:1], jnp.broadcast_to(ml[:, DIM // 2 : DIM // 2 + 1], ml.shape)


def band_kernel(heat_ref, place_ref, q_ref, k_ref, v_ref, *refs):
    *outs, wide_ref = refs
    log_place = jnp.log(1.0 + place_ref[...].astype(F32))
    rows = [1.0 + heat_ref[h] * log_place for h in range(HEADS)]
    scale = jnp.concatenate(rows * (8 // HEADS), axis=0).T * (math.log2(math.e) / math.sqrt(DIM))
    for w, ref in enumerate((q_ref, k_ref, v_ref)):
        wide_ref[w] = ref[...].astype(F32)
    inner = [lax.broadcasted_iota(jnp.int32, (STRIDE, STRIDE), d) for d in range(2)]
    bias = jnp.where(inner[0] >= inner[1], 0.0, NEG)
    for h in range(HEADS):
        q, k, v = (wide_ref[w, pl.ds(h, STRIDE, stride=HEADS), :] for w in range(3))
        q = q * scale[:, h : h + 1]
        high = q.astype(BF16)
        low = (q - high.astype(F32)).astype(BF16)
        q = jnp.concatenate([high, low], axis=1)
        m, l, acc = attend(q, (k.astype(BF16),), (v.astype(BF16),), (bias,), None, None, None)
        qs_ref, acc_ref, ml_ref = outs[3 * (h // GROUP) :][:3]
        qs_ref[h % GROUP] = q
        acc_ref[h % GROUP] = acc
        ml_ref[h % GROUP] = pack_stats(m, l)


def band(heat, places, q, k, v):
    tokens = BLOCKS * STRIDE
    rows = pl.BlockSpec((STRIDE * HEADS, DIM), lambda j: (j, 0))
    out = lambda d: pl.BlockSpec((GROUP, STRIDE, d), lambda j: (0, j, 0))
    shape = lambda d, t: jax.ShapeDtypeStruct((GROUP, tokens, d), t)
    return pl.pallas_call(
        band_kernel,
        grid=(BLOCKS,),
        in_specs=[
            pl.BlockSpec(memory_space=pltpu.SMEM),
            pl.BlockSpec((1, STRIDE), lambda j: (0, j)),
            rows, rows, rows,
        ],
        out_specs=[out(2 * DIM), out(DIM), out(DIM)] * 2,
        out_shape=[shape(2 * DIM, BF16), shape(DIM, F32), shape(DIM, F32)] * 2,
        scratch_shapes=[pltpu.VMEM((3, STRIDE * HEADS, DIM), F32)],
        compiler_params=pltpu.CompilerParams(vmem_limit_bytes=60 << 20),
        cost_estimate=pl.CostEstimate(
            flops=4 * HEADS * tokens * STRIDE * DIM * 2, bytes_accessed=20 << 20,
            transcendentals=HEADS * tokens * STRIDE,
        ),
        name="band",
    )(heat, places, q, k, v)


def attend_blocks(q_ref, kv_refs, biases, acc_ref, ml_ref, put):
    flat = lambda ref: ref[...].reshape(CHIPS * COLS, DIM)
    keys = [flat(k) for k, _ in kv_refs]
    values = [flat(v) for _, v in kv_refs]
    for j in range(BLOCKS):
        rows = pl.ds(j * STRIDE, STRIDE)
        m, l = unpack_stats(ml_ref[0, rows, :])
        put(j, *attend(q_ref[0, rows, :], keys, values, biases(j), m, l, acc_ref[0, rows, :]))


def own_biases():
    z, core = lax.axis_index("z"), lax.axis_index("core")
    col = lax.broadcasted_iota(jnp.int32, (1, CHIPS * COLS), 1)
    other = jnp.where(col < (z + core) * COLS, 0.0, NEG)
    return lambda j: [jnp.where(col < z * COLS + SUMM * j, 0.0, NEG), other]


def no_biases(j):
    return [None, None]


def summary_kernel(own, far, q_ref, *refs):
    kv_refs, refs = refs[: 4 * (own + far)], refs[4 * (own + far) :]
    acc_ref, ml_ref, *outs = refs
    kv = [(kv_refs[i], kv_refs[i + 2]) for s in range(own + far) for i in (4 * s, 4 * s + 1)]

    def keep(j, m, l, acc):
        rows = pl.ds(j * STRIDE, STRIDE)
        outs[0][0, rows, :] = acc
        outs[1][0, rows, :] = pack_stats(m, l)

    def finish(j, m, l, acc):
        outs[0][j, 0] = (acc / l).astype(BF16)

    if not far:
        attend_blocks(q_ref, kv, own_biases(), acc_ref, ml_ref, keep)
        return

    @pl.when(lax.axis_index("x_lo") == 1)
    def _():
        near = own_biases() if own else lambda j: []
        attend_blocks(q_ref, kv, lambda j: near(j) + [None, None], acc_ref, ml_ref, finish)

    @pl.when(lax.axis_index("x_lo") == 0)
    def _():
        if own:
            attend_blocks(q_ref, kv[:2], own_biases(), acc_ref, ml_ref, finish)
        else:
            for j in range(BLOCKS):
                rows = pl.ds(j * STRIDE, STRIDE)
                m, l = unpack_stats(ml_ref[0, rows, :])
                finish(j, m, l, acc_ref[0, rows, :])


def summaries(q, acc, ml, own=(), far=()):
    tokens = BLOCKS * STRIDE
    kv = lambda w: pl.BlockSpec((CHIPS, 1, 1, COLS, DIM), lambda h: (0, w, h, 0, 0))
    state = lambda d: pl.BlockSpec((1, tokens, d), lambda h: (h, 0, 0))
    sets = [s for s in (own, far) if s]
    if far:
        out_specs = pl.BlockSpec((BLOCKS, 1, STRIDE, DIM), lambda h: (0, h, 0, 0))
        out_shape = jax.ShapeDtypeStruct((BLOCKS, GROUP, STRIDE, DIM), BF16)
    else:
        out_specs = [state(DIM)] * 2
        out_shape = [jax.ShapeDtypeStruct((GROUP, tokens, DIM), F32)] * 2
    work = GROUP * tokens * 2 * CHIPS * COLS * len(sets) // 64
    return pl.pallas_call(
        functools.partial(summary_kernel, bool(own), bool(far)),
        grid=(GROUP,),
        in_specs=[
            state(2 * DIM),
            *[kv(0), kv(0), kv(1), kv(1)] * len(sets),
            state(DIM), state(DIM),
        ],
        out_specs=out_specs,
        out_shape=out_shape,
        compiler_params=pltpu.CompilerParams(vmem_limit_bytes=60 << 20),
        cost_estimate=pl.CostEstimate(
            flops=8 * work * DIM, bytes_accessed=work // 4, transcendentals=work
        ),
        name="_".join(n for n, s in (("own", own), ("far", far)) if s),
    )(q, *[x for mine, other in sets for x in (mine, other) * 2], acc, ml)


def assemble_kernel(x0_ref, x1_ref, out_ref):
    heads = [(x0_ref, x1_ref)[h // GROUP][s, h % GROUP] for s in range(BLOCKS) for h in range(HEADS)]
    out_ref[...] = jnp.swapaxes(jnp.stack(heads), 0, 1)


def assemble(x0, x1, steps=4):
    count = STRIDE // steps
    total = BLOCKS * HEADS
    spec = pl.BlockSpec((BLOCKS, GROUP, count, DIM), lambda t: (0, 0, t, 0))
    return pl.pallas_call(
        assemble_kernel,
        grid=(steps,),
        in_specs=[spec, spec],
        out_specs=pl.BlockSpec((count, total, DIM), lambda t: (t, 0, 0)),
        out_shape=jax.ShapeDtypeStruct((STRIDE, total, DIM), BF16),
        compiler_params=pltpu.CompilerParams(vmem_limit_bytes=60 << 20),
        name="assemble",
    )(x0, x1)


def after(value, *done):
    return lax.optimization_barrier((value, *done))[0]


def per_device(q, k, v, heat, places, shifts):
    tokens = BLOCKS * STRIDE
    swap, up = [(0, 1), (1, 0)], [(0, 1)]
    flat = lambda x: x.reshape(tokens * HEADS, DIM)
    spread = lambda x: lax.all_to_all(x, "z", 0, 0, tiled=True)
    give = lambda x: lax.all_to_all(x, HEAD, 0, 0, tiled=True)

    send0, send1 = gather_summaries(shifts, k, v)
    mine0 = spread(send0)
    qs0, acc0, ml0, qs1, acc1, ml1 = band(heat, places.reshape(1, tokens), flat(q), flat(k), flat(v))
    mine0 = after(mine0, ml0)
    mine1 = spread(after(send1, mine0))
    other0 = lax.ppermute(mine0, "core", swap)
    far0 = lax.ppermute(mine0, "x_lo", up)
    state0 = summaries(qs0, acc0, ml0, own=(mine0, other0))
    far0 = after(far0, state0[1])
    far_other0 = lax.ppermute(far0, "core", swap)
    part0 = summaries(qs0, *state0, far=(far0, far_other0))
    out0 = give(part0)
    mine1 = after(mine1, part0)
    other1 = lax.ppermute(mine1, "core", swap)
    far1 = lax.ppermute(mine1, "x_lo", up)
    state1 = summaries(qs1, after(acc1, part0), ml1, own=(mine1, other1))
    far1 = after(far1, state1[1])
    far_other1 = lax.ppermute(far1, "core", swap)
    part1 = summaries(qs1, *state1, far=(far1, far_other1))
    out1 = give(after(part1, out0))
    return assemble(out0, out1)


def solution(mesh):
    devices = mesh.devices
    wide = Mesh(devices.reshape(2, 8, 2, 2, 4), CTX + HEAD)
    in_specs = (
        P(CTX, HEAD, None),
        P(CTX, HEAD, None),
        P(CTX, HEAD, None),
        P(HEAD),
        P(CTX),
        P(CTX, None),
    )
    return jax.shard_map(
        per_device, mesh=wide, in_specs=in_specs, out_specs=P(CTX + HEAD, None, None),
        check_vma=False,
    )
```

```python
import functools
import math

import jax
import jax.numpy as jnp
from jax import lax
from jax.experimental import pallas as pl
from jax.experimental.pallas import tpu as pltpu
from jax.sharding import Mesh
from jax.sharding import PartitionSpec as P

F32, BF16 = jnp.float32, jnp.bfloat16
NEG = -1e30
STRIDE, SUMM, DIM, HEADS = 256, 8, 128, 4
BLOCKS = 8
COLS = BLOCKS * SUMM
CHIPS = 8
GROUP = 2
TRANS_B = (((1,), (1,)), ((), ()))
CTX = ("x_lo", "z", "core")
HEAD = ("x_hi", "y")


def gather_kernel(shift_ref, k_hbm, v_hbm, out0_ref, out1_ref, rows_ref, wide_ref, sems):
    for w, hbm in enumerate((k_hbm, v_hbm)):
        for c in range(COLS):
            row = (c // SUMM) * STRIDE + shift_ref[c // SUMM, c % SUMM]
            pltpu.make_async_copy(
                hbm.at[pl.ds(row, 1)], rows_ref.at[w, pl.ds(c, 1)], sems.at[w]
            ).start()
    for w, hbm in enumerate((k_hbm, v_hbm)):
        pltpu.make_async_copy(hbm.at[pl.ds(0, COLS)], rows_ref.at[w], sems.at[w]).wait()
        for c in range(COLS):
            wide_ref[w, pl.ds(c * HEADS, HEADS), :] = rows_ref[w, c].astype(F32)
        for h in range(HEADS):
            out_ref = (out0_ref, out1_ref)[h // GROUP]
            x = wide_ref[w, pl.ds(h, COLS, stride=HEADS), :].astype(BF16)
            for d in range(CHIPS):
                out_ref[d, w, h % GROUP] = x


def gather_summaries(digest_shifts, keys, values):
    out = jax.ShapeDtypeStruct((CHIPS, 2, GROUP, COLS, DIM), BF16)
    return pl.pallas_call(
        gather_kernel,
        in_specs=[
            pl.BlockSpec(memory_space=pltpu.SMEM),
            pl.BlockSpec(memory_space=pl.ANY),
            pl.BlockSpec(memory_space=pl.ANY),
        ],
        out_shape=[out, out],
        scratch_shapes=[
            pltpu.VMEM((2, COLS, HEADS, DIM), BF16),
            pltpu.VMEM((2, COLS * HEADS, DIM), F32),
            pltpu.SemaphoreType.DMA((2,)),
        ],
        name="gather_summaries",
    )(digest_shifts, keys, values)


def attend(q, keys, values, biases, m, l, acc):
    scores = []
    for k, bias in zip(keys, biases):
        s = lax.dot_general(
            q, jnp.concatenate([k, k], axis=1), TRANS_B, preferred_element_type=F32
        )
        scores.append(s if bias is None else s + bias)
    top = m
    for s in scores:
        peak = s.max(axis=1, keepdims=True)
        top = peak if top is None else jnp.maximum(top, peak)
    if m is not None:
        shrink = jnp.exp2(m - top)
        acc, l = acc * shrink, l * shrink
    for s, v in zip(scores, values):
        p = jnp.exp2(s - top).astype(BF16)
        o = jnp.dot(
            p, jnp.concatenate([v, jnp.ones_like(v)], axis=1), preferred_element_type=F32
        )
        acc = o[:, :DIM] if acc is None else acc + o[:, :DIM]
        l = o[:, DIM:] if l is None else l + o[:, DIM:]
    return top, l, acc


def pack_stats(m, l):
    lane = lax.broadcasted_iota(jnp.int32, l.shape, 1)
    return jnp.where(lane < DIM // 2, m, l)


def unpack_stats(ml):
    return ml[:, 0:1], jnp.broadcast_to(ml[:, DIM // 2 : DIM // 2 + 1], ml.shape)


def band_kernel(heat_ref, place_ref, q_ref, k_ref, v_ref, *refs):
    *outs, wide_ref = refs
    log_place = jnp.log(1.0 + place_ref[...].astype(F32))
    rows = [1.0 + heat_ref[h] * log_place for h in range(HEADS)]
    scale = jnp.concatenate(rows * (8 // HEADS), axis=0).T * (math.log2(math.e) / math.sqrt(DIM))
    for w, ref in enumerate((q_ref, k_ref, v_ref)):
        wide_ref[w] = ref[...].astype(F32)
    inner = [lax.broadcasted_iota(jnp.int32, (STRIDE, STRIDE), d) for d in range(2)]
    bias = jnp.where(inner[0] >= inner[1], 0.0, NEG)
    for h in range(HEADS):
        q, k, v = (wide_ref[w, pl.ds(h, STRIDE, stride=HEADS), :] for w in range(3))
        q = q * scale[:, h : h + 1]
        high = q.astype(BF16)
        low = (q - high.astype(F32)).astype(BF16)
        q = jnp.concatenate([high, low], axis=1)
        m, l, acc = attend(q, (k.astype(BF16),), (v.astype(BF16),), (bias,), None, None, None)
        qs_ref, acc_ref, ml_ref = outs[3 * (h // GROUP) :][:3]
        qs_ref[h % GROUP] = q
        acc_ref[h % GROUP] = acc
        ml_ref[h % GROUP] = pack_stats(m, l)


def band(heat, places, q, k, v):
    tokens = BLOCKS * STRIDE
    rows = pl.BlockSpec((STRIDE * HEADS, DIM), lambda j: (j, 0))
    out = lambda d: pl.BlockSpec((GROUP, STRIDE, d), lambda j: (0, j, 0))
    shape = lambda d, t: jax.ShapeDtypeStruct((GROUP, tokens, d), t)
    return pl.pallas_call(
        band_kernel,
        grid=(BLOCKS,),
        in_specs=[
            pl.BlockSpec(memory_space=pltpu.SMEM),
            pl.BlockSpec((1, STRIDE), lambda j: (0, j)),
            rows, rows, rows,
        ],
        out_specs=[out(2 * DIM), out(DIM), out(DIM)] * 2,
        out_shape=[shape(2 * DIM, BF16), shape(DIM, F32), shape(DIM, F32)] * 2,
        scratch_shapes=[pltpu.VMEM((3, STRIDE * HEADS, DIM), F32)],
        compiler_params=pltpu.CompilerParams(vmem_limit_bytes=67_000_000),
        cost_estimate=pl.CostEstimate(
            flops=4 * HEADS * tokens * STRIDE * DIM * 2, bytes_accessed=20 << 20,
            transcendentals=HEADS * tokens * STRIDE,
        ),
        name="band",
    )(heat, places, q, k, v)


def attend_blocks(q_ref, kv_refs, biases, acc_ref, ml_ref, put, chips=CHIPS):
    flat = lambda ref: ref[0:chips].reshape(chips * COLS, DIM)
    keys = [flat(k) for k, _ in kv_refs]
    values = [flat(v) for _, v in kv_refs]
    for j in range(BLOCKS):
        rows = pl.ds(j * STRIDE, STRIDE)
        m, l = unpack_stats(ml_ref[0, rows, :])
        put(j, *attend(q_ref[0, rows, :], keys, values, biases(j), m, l, acc_ref[0, rows, :]))


def own_biases(chips=CHIPS):
    z, core = lax.axis_index("z"), lax.axis_index("core")
    col = lax.broadcasted_iota(jnp.int32, (1, chips * COLS), 1)
    other = jnp.where(col < (z + core) * COLS, 0.0, NEG)
    return lambda j: [jnp.where(col < z * COLS + SUMM * j, 0.0, NEG), other]


def no_biases(j):
    return [None, None]


def summary_kernel(own, far, q_ref, *refs):
    kv_refs, refs = refs[: 4 * (own + far)], refs[4 * (own + far) :]
    acc_ref, ml_ref, *outs = refs
    kv = [(kv_refs[i], kv_refs[i + 2]) for s in range(own + far) for i in (4 * s, 4 * s + 1)]

    def keep(j, m, l, acc):
        rows = pl.ds(j * STRIDE, STRIDE)
        outs[0][0, rows, :] = acc
        outs[1][0, rows, :] = pack_stats(m, l)

    def finish(j, m, l, acc):
        outs[0][j, 0] = (acc / l).astype(BF16)

    if not far:
        low = lax.axis_index("z") < CHIPS // 2
        for chips, here in ((CHIPS // 2, low), (CHIPS, jnp.logical_not(low))):

            @pl.when(here)
            def _(chips=chips):
                attend_blocks(q_ref, kv, own_biases(chips), acc_ref, ml_ref, keep, chips)

        return

    @pl.when(lax.axis_index("x_lo") == 1)
    def _():
        near = own_biases() if own else lambda j: []
        attend_blocks(q_ref, kv, lambda j: near(j) + [None, None], acc_ref, ml_ref, finish)

    @pl.when(lax.axis_index("x_lo") == 0)
    def _():
        if own:
            attend_blocks(q_ref, kv[:2], own_biases(), acc_ref, ml_ref, finish)
        else:
            for j in range(BLOCKS):
                rows = pl.ds(j * STRIDE, STRIDE)
                m, l = unpack_stats(ml_ref[0, rows, :])
                finish(j, m, l, acc_ref[0, rows, :])


def summaries(q, acc, ml, own=(), far=()):
    tokens = BLOCKS * STRIDE
    kv = lambda w: pl.BlockSpec((CHIPS, 1, 1, COLS, DIM), lambda h: (0, w, h, 0, 0))
    state = lambda d: pl.BlockSpec((1, tokens, d), lambda h: (h, 0, 0))
    sets = [s for s in (own, far) if s]
    if far:
        out_specs = pl.BlockSpec((BLOCKS, 1, STRIDE, DIM), lambda h: (0, h, 0, 0))
        out_shape = jax.ShapeDtypeStruct((BLOCKS, GROUP, STRIDE, DIM), BF16)
    else:
        out_specs = [state(DIM)] * 2
        out_shape = [jax.ShapeDtypeStruct((GROUP, tokens, DIM), F32)] * 2
    work = GROUP * tokens * 2 * CHIPS * COLS * len(sets) // 64
    return pl.pallas_call(
        functools.partial(summary_kernel, bool(own), bool(far)),
        grid=(GROUP,),
        in_specs=[
            state(2 * DIM),
            *[kv(0), kv(0), kv(1), kv(1)] * len(sets),
            state(DIM), state(DIM),
        ],
        out_specs=out_specs,
        out_shape=out_shape,
        compiler_params=pltpu.CompilerParams(vmem_limit_bytes=67_000_000),
        cost_estimate=pl.CostEstimate(
            flops=8 * work * DIM, bytes_accessed=work // 4, transcendentals=work
        ),
        name="_".join(n for n, s in (("own", own), ("far", far)) if s),
    )(q, *[x for mine, other in sets for x in (mine, other) * 2], acc, ml)


def assemble_kernel(x0_ref, x1_ref, out_ref):
    heads = [(x0_ref, x1_ref)[h // GROUP][s, h % GROUP] for s in range(BLOCKS) for h in range(HEADS)]
    out_ref[...] = jnp.swapaxes(jnp.stack(heads), 0, 1)


def assemble(x0, x1, steps=4):
    count = STRIDE // steps
    total = BLOCKS * HEADS
    spec = pl.BlockSpec((BLOCKS, GROUP, count, DIM), lambda t: (0, 0, t, 0))
    return pl.pallas_call(
        assemble_kernel,
        grid=(steps,),
        in_specs=[spec, spec],
        out_specs=pl.BlockSpec((count, total, DIM), lambda t: (t, 0, 0)),
        out_shape=jax.ShapeDtypeStruct((STRIDE, total, DIM), BF16),
        compiler_params=pltpu.CompilerParams(vmem_limit_bytes=67_000_000),
        name="assemble",
    )(x0, x1)


def after(value, *done):
    return lax.optimization_barrier((value, *done))[0]


def per_device(q, k, v, heat, places, shifts):
    tokens = BLOCKS * STRIDE
    swap, up = [(0, 1), (1, 0)], [(0, 1)]
    flat = lambda x: x.reshape(tokens * HEADS, DIM)
    spread = lambda x: lax.all_to_all(x, "z", 0, 0, tiled=True)
    give = lambda x: lax.all_to_all(x, HEAD, 0, 0, tiled=True)

    send0, send1 = gather_summaries(shifts, k, v)
    mine0 = spread(send0)
    qs0, acc0, ml0, qs1, acc1, ml1 = band(heat, places.reshape(1, tokens), flat(q), flat(k), flat(v))
    mine0 = after(mine0, ml0)
    mine1 = spread(after(send1, mine0))
    other0 = lax.ppermute(mine0, "core", swap)
    far0 = lax.ppermute(mine0, "x_lo", up)
    state0 = summaries(qs0, acc0, ml0, own=(mine0, other0))
    far0 = after(far0, state0[1])
    far_other0 = lax.ppermute(far0, "core", swap)
    part0 = summaries(qs0, *state0, far=(far0, far_other0))
    out0 = give(part0)
    mine1 = after(mine1, part0)
    other1 = lax.ppermute(mine1, "core", swap)
    far1 = lax.ppermute(mine1, "x_lo", up)
    state1 = summaries(qs1, after(acc1, part0), ml1, own=(mine1, other1))
    far1 = after(far1, state1[1])
    far_other1 = lax.ppermute(far1, "core", swap)
    part1 = summaries(qs1, *state1, far=(far1, far_other1))
    out1 = give(after(part1, out0))
    return assemble(out0, out1)


def solution(mesh):
    devices = mesh.devices
    wide = Mesh(devices.reshape(2, 8, 2, 2, 4), CTX + HEAD)
    in_specs = (
        P(CTX, HEAD, None),
        P(CTX, HEAD, None),
        P(CTX, HEAD, None),
        P(HEAD),
        P(CTX),
        P(CTX, None),
    )
    return jax.shard_map(
        per_device, mesh=wide, in_specs=in_specs, out_specs=P(CTX + HEAD, None, None),
        check_vma=False,
    )
```

```python
import functools
import math

import jax
import jax.numpy as jnp
from jax import lax
from jax.experimental import pallas as pl
from jax.experimental.pallas import tpu as pltpu
from jax.sharding import Mesh
from jax.sharding import PartitionSpec as P

F32, BF16 = jnp.float32, jnp.bfloat16
NEG = -1e30
STRIDE, SUMM, DIM, HEADS = 256, 8, 128, 4
BLOCKS = 8
COLS = BLOCKS * SUMM
CHIPS = 8
GROUP = 2
TRANS_B = (((1,), (1,)), ((), ()))
CTX = ("x_lo", "z", "core")
HEAD = ("x_hi", "y")


def gather_kernel(shift_ref, k_hbm, v_hbm, out0_ref, out1_ref, rows_ref, wide_ref, sems):
    for w, hbm in enumerate((k_hbm, v_hbm)):
        for c in range(COLS):
            row = (c // SUMM) * STRIDE + shift_ref[c // SUMM, c % SUMM]
            pltpu.make_async_copy(
                hbm.at[pl.ds(row, 1)], rows_ref.at[w, pl.ds(c, 1)], sems.at[w]
            ).start()
    for w, hbm in enumerate((k_hbm, v_hbm)):
        pltpu.make_async_copy(hbm.at[pl.ds(0, COLS)], rows_ref.at[w], sems.at[w]).wait()
        for c in range(COLS):
            wide_ref[w, pl.ds(c * HEADS, HEADS), :] = rows_ref[w, c].astype(F32)
        for h in range(HEADS):
            out_ref = (out0_ref, out1_ref)[h // GROUP]
            x = wide_ref[w, pl.ds(h, COLS, stride=HEADS), :].astype(BF16)
            for d in range(CHIPS):
                out_ref[d, w, h % GROUP] = x


def gather_summaries(digest_shifts, keys, values):
    out = jax.ShapeDtypeStruct((CHIPS, 2, GROUP, COLS, DIM), BF16)
    return pl.pallas_call(
        gather_kernel,
        in_specs=[
            pl.BlockSpec(memory_space=pltpu.SMEM),
            pl.BlockSpec(memory_space=pl.ANY),
            pl.BlockSpec(memory_space=pl.ANY),
        ],
        out_shape=[out, out],
        scratch_shapes=[
            pltpu.VMEM((2, COLS, HEADS, DIM), BF16),
            pltpu.VMEM((2, COLS * HEADS, DIM), F32),
            pltpu.SemaphoreType.DMA((2,)),
        ],
        name="gather_summaries",
    )(digest_shifts, keys, values)


def score(q, keys, biases):
    scores = []
    for k, bias in zip(keys, biases):
        s = lax.dot_general(
            q, jnp.concatenate([k, k], axis=1), TRANS_B, preferred_element_type=F32
        )
        scores.append(s if bias is None else s + bias)
    return scores


def attend(scores, values, m, l, acc):
    top = m
    for s in scores:
        peak = s.max(axis=1, keepdims=True)
        top = peak if top is None else jnp.maximum(top, peak)
    if m is not None:
        shrink = jnp.exp2(m - top)
        acc, l = acc * shrink, l * shrink
    for s, v in zip(scores, values):
        p = jnp.exp2(s - top).astype(BF16)
        o = jnp.dot(
            p, jnp.concatenate([v, jnp.ones_like(v)], axis=1), preferred_element_type=F32
        )
        acc = o[:, :DIM] if acc is None else acc + o[:, :DIM]
        l = o[:, DIM:] if l is None else l + o[:, DIM:]
    return top, l, acc


def pack_stats(m, l):
    lane = lax.broadcasted_iota(jnp.int32, l.shape, 1)
    return jnp.where(lane < DIM // 2, m, l)


def unpack_stats(ml):
    return ml[:, 0:1], jnp.broadcast_to(ml[:, DIM // 2 : DIM // 2 + 1], ml.shape)


def band_kernel(heat_ref, place_ref, q_ref, k_ref, v_ref, *refs):
    *outs, wide_ref = refs
    log_place = jnp.log(1.0 + place_ref[...].astype(F32))
    rows = [1.0 + heat_ref[h] * log_place for h in range(HEADS)]
    scale = jnp.concatenate(rows * (8 // HEADS), axis=0).T * (math.log2(math.e) / math.sqrt(DIM))
    for w, ref in enumerate((q_ref, k_ref, v_ref)):
        wide_ref[w] = ref[...].astype(F32)
    inner = [lax.broadcasted_iota(jnp.int32, (STRIDE, STRIDE), d) for d in range(2)]
    bias = jnp.where(inner[0] >= inner[1], 0.0, NEG)
    queries, scores, values = [], [], []
    for h in range(HEADS):
        q, k, v = (wide_ref[w, pl.ds(h, STRIDE, stride=HEADS), :] for w in range(3))
        q = q * scale[:, h : h + 1]
        high = q.astype(BF16)
        low = (q - high.astype(F32)).astype(BF16)
        queries.append(jnp.concatenate([high, low], axis=1))
        scores.append(score(queries[h], (k.astype(BF16),), (bias,)))
        values.append(v.astype(BF16))
    for h in range(HEADS):
        m, l, acc = attend(scores[h], (values[h],), None, None, None)
        qs_ref, acc_ref, ml_ref = outs[3 * (h // GROUP) :][:3]
        qs_ref[h % GROUP] = queries[h]
        acc_ref[h % GROUP] = acc
        ml_ref[h % GROUP] = pack_stats(m, l)


def band(heat, places, q, k, v):
    tokens = BLOCKS * STRIDE
    rows = pl.BlockSpec((STRIDE * HEADS, DIM), lambda j: (j, 0))
    out = lambda d: pl.BlockSpec((GROUP, STRIDE, d), lambda j: (0, j, 0))
    shape = lambda d, t: jax.ShapeDtypeStruct((GROUP, tokens, d), t)
    return pl.pallas_call(
        band_kernel,
        grid=(BLOCKS,),
        in_specs=[
            pl.BlockSpec(memory_space=pltpu.SMEM),
            pl.BlockSpec((1, STRIDE), lambda j: (0, j)),
            rows, rows, rows,
        ],
        out_specs=[out(2 * DIM), out(DIM), out(DIM)] * 2,
        out_shape=[shape(2 * DIM, BF16), shape(DIM, F32), shape(DIM, F32)] * 2,
        scratch_shapes=[pltpu.VMEM((3, STRIDE * HEADS, DIM), F32)],
        compiler_params=pltpu.CompilerParams(vmem_limit_bytes=67_000_000),
        cost_estimate=pl.CostEstimate(
            flops=4 * HEADS * tokens * STRIDE * DIM * 2, bytes_accessed=20 << 20,
            transcendentals=HEADS * tokens * STRIDE,
        ),
        name="band",
    )(heat, places, q, k, v)


def attend_blocks(q_ref, kv_refs, biases, acc_ref, ml_ref, put, chips=CHIPS):
    flat = lambda ref: ref[0:chips].reshape(chips * COLS, DIM)
    keys = [flat(k) for k, _ in kv_refs]
    values = [flat(v) for _, v in kv_refs]
    scores = lambda j: score(q_ref[0, pl.ds(j * STRIDE, STRIDE), :], keys, biases(j))
    ahead = scores(0)
    for j in range(BLOCKS):
        now, ahead = ahead, scores(j + 1) if j + 1 < BLOCKS else None
        rows = pl.ds(j * STRIDE, STRIDE)
        m, l = unpack_stats(ml_ref[0, rows, :])
        put(j, *attend(now, values, m, l, acc_ref[0, rows, :]))


def own_biases(chips=CHIPS):
    z, core = lax.axis_index("z"), lax.axis_index("core")
    col = lax.broadcasted_iota(jnp.int32, (1, chips * COLS), 1)
    other = jnp.where(col < (z + core) * COLS, 0.0, NEG)
    return lambda j: [jnp.where(col < z * COLS + SUMM * j, 0.0, NEG), other]


def no_biases(j):
    return [None, None]


def summary_kernel(own, far, q_ref, *refs):
    kv_refs, refs = refs[: 4 * (own + far)], refs[4 * (own + far) :]
    acc_ref, ml_ref, *outs = refs
    kv = [(kv_refs[i], kv_refs[i + 2]) for s in range(own + far) for i in (4 * s, 4 * s + 1)]

    def keep(j, m, l, acc):
        rows = pl.ds(j * STRIDE, STRIDE)
        outs[0][0, rows, :] = acc
        outs[1][0, rows, :] = pack_stats(m, l)

    def finish(j, m, l, acc):
        outs[0][j, 0] = (acc / l).astype(BF16)

    if not far:
        low = lax.axis_index("z") < CHIPS // 2
        for chips, here in ((CHIPS // 2, low), (CHIPS, jnp.logical_not(low))):

            @pl.when(here)
            def _(chips=chips):
                attend_blocks(q_ref, kv, own_biases(chips), acc_ref, ml_ref, keep, chips)

        return

    @pl.when(lax.axis_index("x_lo") == 1)
    def _():
        near = own_biases() if own else lambda j: []
        attend_blocks(q_ref, kv, lambda j: near(j) + [None, None], acc_ref, ml_ref, finish)

    @pl.when(lax.axis_index("x_lo") == 0)
    def _():
        if own:
            attend_blocks(q_ref, kv[:2], own_biases(), acc_ref, ml_ref, finish)
        else:
            for j in range(BLOCKS):
                rows = pl.ds(j * STRIDE, STRIDE)
                m, l = unpack_stats(ml_ref[0, rows, :])
                finish(j, m, l, acc_ref[0, rows, :])


def summaries(q, acc, ml, own=(), far=()):
    tokens = BLOCKS * STRIDE
    kv = lambda w: pl.BlockSpec((CHIPS, 1, 1, COLS, DIM), lambda h: (0, w, h, 0, 0))
    state = lambda d: pl.BlockSpec((1, tokens, d), lambda h: (h, 0, 0))
    sets = [s for s in (own, far) if s]
    if far:
        out_specs = pl.BlockSpec((BLOCKS, 1, STRIDE, DIM), lambda h: (0, h, 0, 0))
        out_shape = jax.ShapeDtypeStruct((BLOCKS, GROUP, STRIDE, DIM), BF16)
    else:
        out_specs = [state(DIM)] * 2
        out_shape = [jax.ShapeDtypeStruct((GROUP, tokens, DIM), F32)] * 2
    work = GROUP * tokens * 2 * CHIPS * COLS * len(sets) // 64
    return pl.pallas_call(
        functools.partial(summary_kernel, bool(own), bool(far)),
        grid=(GROUP,),
        in_specs=[
            state(2 * DIM),
            *[kv(0), kv(0), kv(1), kv(1)] * len(sets),
            state(DIM), state(DIM),
        ],
        out_specs=out_specs,
        out_shape=out_shape,
        compiler_params=pltpu.CompilerParams(vmem_limit_bytes=67_000_000),
        cost_estimate=pl.CostEstimate(
            flops=8 * work * DIM, bytes_accessed=work // 4, transcendentals=work
        ),
        name="_".join(n for n, s in (("own", own), ("far", far)) if s),
    )(q, *[x for mine, other in sets for x in (mine, other) * 2], acc, ml)


def assemble_kernel(x0_ref, x1_ref, out_ref):
    heads = [(x0_ref, x1_ref)[h // GROUP][s, h % GROUP] for s in range(BLOCKS) for h in range(HEADS)]
    out_ref[...] = jnp.swapaxes(jnp.stack(heads), 0, 1)


def assemble(x0, x1, steps=4):
    count = STRIDE // steps
    total = BLOCKS * HEADS
    spec = pl.BlockSpec((BLOCKS, GROUP, count, DIM), lambda t: (0, 0, t, 0))
    return pl.pallas_call(
        assemble_kernel,
        grid=(steps,),
        in_specs=[spec, spec],
        out_specs=pl.BlockSpec((count, total, DIM), lambda t: (t, 0, 0)),
        out_shape=jax.ShapeDtypeStruct((STRIDE, total, DIM), BF16),
        compiler_params=pltpu.CompilerParams(vmem_limit_bytes=67_000_000),
        name="assemble",
    )(x0, x1)


def after(value, *done):
    return lax.optimization_barrier((value, *done))[0]


def per_device(q, k, v, heat, places, shifts):
    tokens = BLOCKS * STRIDE
    swap, up = [(0, 1), (1, 0)], [(0, 1)]
    flat = lambda x: x.reshape(tokens * HEADS, DIM)
    spread = lambda x: lax.all_to_all(x, "z", 0, 0, tiled=True)
    give = lambda x: lax.all_to_all(x, HEAD, 0, 0, tiled=True)

    send0, send1 = gather_summaries(shifts, k, v)
    mine0 = spread(send0)
    qs0, acc0, ml0, qs1, acc1, ml1 = band(heat, places.reshape(1, tokens), flat(q), flat(k), flat(v))
    mine0 = after(mine0, ml0)
    mine1 = spread(after(send1, mine0))
    other0 = lax.ppermute(mine0, "core", swap)
    far0 = lax.ppermute(mine0, "x_lo", up)
    state0 = summaries(qs0, acc0, ml0, own=(mine0, other0))
    far0 = after(far0, state0[1])
    far_other0 = lax.ppermute(far0, "core", swap)
    part0 = summaries(qs0, *state0, far=(far0, far_other0))
    out0 = give(part0)
    mine1 = after(mine1, part0)
    other1 = lax.ppermute(mine1, "core", swap)
    far1 = lax.ppermute(mine1, "x_lo", up)
    state1 = summaries(qs1, after(acc1, part0), ml1, own=(mine1, other1))
    far1 = after(far1, state1[1])
    far_other1 = lax.ppermute(far1, "core", swap)
    part1 = summaries(qs1, *state1, far=(far1, far_other1))
    out1 = give(after(part1, out0))
    return assemble(out0, out1)


def solution(mesh):
    devices = mesh.devices
    wide = Mesh(devices.reshape(2, 8, 2, 2, 4), CTX + HEAD)
    in_specs = (
        P(CTX, HEAD, None),
        P(CTX, HEAD, None),
        P(CTX, HEAD, None),
        P(HEAD),
        P(CTX),
        P(CTX, None),
    )
    return jax.shard_map(
        per_device, mesh=wide, in_specs=in_specs, out_specs=P(CTX + HEAD, None, None),
        check_vma=False,
    )
```
